32 devices in a mesh: lat: 4 (over y, x), lon: 8 (over z, core).
Axes of the slice: x: 2, y: 2, z: 4, core: 2. Of those that a mesh axis runs over, the one named last changes fastest.
Arguments:
- fine: bfloat16 [4, 48, 192, 512], P(None, 'lat', 'lon'), may hold values from -6 to 6
- fine_qkv: bfloat16 [512, 1536], replicated
- fine_out: bfloat16 [512, 512], replicated, may hold values from -0.25 to 0.25
- fine_up: bfloat16 [512, 2048], replicated, may hold values from -0.25 to 0.25
- fine_down: bfloat16 [2048, 512], replicated, may hold values from -0.125 to 0.125
- merge_weight: bfloat16 [2048, 1024], replicated, may hold values from -0.125 to 0.125
- coarse_qkv: bfloat16 [1024, 3072], replicated
- coarse_out: bfloat16 [1024, 1024], replicated, may hold values from -0.1875 to 0.1875
Outputs:
- coarse: bfloat16 [4, 24, 96, 1024], P(None, 'lat', 'lon')
The draws below stay inside these ranges and needn't reach their ends.
All inputs are finite; a program needn't handle non-finite values.
Results may differ from the reference program's by a relative error of at most 0.02.
Values may be sent and summed in bfloat16 or wider, within the bound.
A program may use at most 192 MiB of HBM per device.

```python
import jax
import jax.numpy as jnp
from jax import lax

C = 512
HEADS = 16
FF = 2048
C2 = 1024
HEADS2 = 32
NLAT = 48
NLON = 192


def lined_weight(key, width, heads, boost):
    first, second = jax.random.split(key)
    base = jnp.clip(jax.random.normal(first, (width, 3 * width), jnp.float32), -6.0, 6.0) * width ** (-0.5)
    size = width // heads
    head_of = jnp.arange(width) // size
    strength = jax.random.uniform(second, (heads,), jnp.float32, 0.5, 2.0) * boost
    chosen = (head_of % 4 == 0) & (boost > 0)
    query = base[:, :width]
    keys = jnp.where(chosen[None, :], query * strength[head_of][None, :], base[:, width:2 * width])
    return jnp.concatenate([query, keys, base[:, 2 * width:]], 1).astype(jnp.bfloat16)


def draw_fine_qkv(key, part):
    key = jax.random.fold_in(key, 1)
    boost = 0.0
    return lined_weight(key, C, HEADS, boost)


def draw_coarse_qkv(key, part):
    key = jax.random.fold_in(key, 2)
    boost = 0.0
    return lined_weight(key, C2, HEADS2, boost)


def block_scale(rng, extent, cuts, low, largest):
    loudness, own = 1.0, jax.random.fold_in(rng, 6)
    for axis_at, parts in cuts:
        heights = jnp.exp(jax.random.uniform(jax.random.fold_in(own, axis_at), (parts,), jnp.float32, low / len(cuts), largest / len(cuts)))
        loudness = loudness * jnp.repeat(heights, extent[axis_at] // parts).reshape([-1 if axis == axis_at else 1 for axis in range(len(extent))])
    return loudness


def noise(key, dims, scale, limit, cuts=(), kind=jnp.bfloat16):
    drawn = jax.random.normal(key, dims, jnp.float32) * scale
    if len(cuts) > 0:
        drawn = block_scale(key, dims, cuts, -0.22, 0.18) * drawn
    return jnp.clip(drawn, min=-limit, max=limit).astype(kind)


def setup_inputs(seed: int = 0) -> dict:
    key_of = jax.random.split(jax.random.key(seed), 9)
    fine = noise(key_of[0], (4, NLAT, NLON, C), 1.0, 6.0, ((1, 4), (2, 8)))
    fine_qkv = draw_fine_qkv(jax.random.fold_in(key_of[8], 71), 0)
    fine_out = noise(key_of[2], (C, C), C ** -0.5, 0.25)
    fine_up = noise(key_of[3], (C, FF), C ** -0.5, 0.25)
    fine_down = noise(key_of[4], (FF, C), FF ** -0.5, 0.125)
    merge_weight = noise(key_of[5], (4 * C, C2), (4 * C) ** -0.5, 0.125)
    coarse_qkv = draw_coarse_qkv(jax.random.fold_in(key_of[8], 71), 0)
    coarse_out = noise(key_of[7], (C2, C2), C2 ** -0.5, 0.1875)
    return {"fine": fine, "fine_qkv": fine_qkv, "fine_out": fine_out, "fine_up": fine_up, "fine_down": fine_down, "merge_weight": merge_weight, "coarse_qkv": coarse_qkv, "coarse_out": coarse_out}


def normalize(values):
    values = values.astype(jnp.float32)
    center = values - lax.optimization_barrier(jnp.mean(values, -1, keepdims=True))
    spread = lax.optimization_barrier(jnp.mean(center * center, -1, keepdims=True))
    return center * lax.rsqrt(spread + 1e-05)

def attend_rows(qkv, lat_valid, heads):
    levels, rows, cols, width = qkv.shape
    chan = width // 3
    size = chan // heads
    row_win = rows // 6
    col_win = cols // 12
    blocks = qkv.reshape(2, 2, row_win, 6, col_win, 12, width).transpose(2, 0, 4, 1, 3, 5, 6)
    blocks = blocks.reshape(row_win, 2 * col_win, 144, width)
    valid_rows = lat_valid.reshape(row_win, 6)
    token = jnp.arange(144)
    level_in = token // 72
    lat_in = token // 12 % 6
    window_level = jnp.arange(2 * col_win) // col_win
    group = jnp.where(window_level[:, None] == 0, 0, 1 + level_in[None, :])
    same = group[:, :, None] == group[:, None, :]

    def one_row(item):
        block, valid = item
        keep = same & valid[lat_in][None, None, :]
        query = block[..., :chan].reshape(-1, 144, heads, size).astype(jnp.float32)
        keys = block[..., chan:2 * chan].reshape(-1, 144, heads, size).astype(jnp.float32)
        values = block[..., 2 * chan:].reshape(-1, 144, heads, size).astype(jnp.float32)
        scores = jnp.einsum('wqhd,wkhd->whqk', query, keys) * size ** (-0.5)
        scores = jnp.where(keep[:, None], scores, -1e+30)
        expo = jnp.exp(scores - lax.optimization_barrier(jnp.max(scores, -1, keepdims=True)))
        weights = (expo / lax.optimization_barrier(jnp.sum(expo, -1, keepdims=True))).astype(jnp.bfloat16)
        attended = jnp.einsum('whqk,wkhd->wqhd', weights.astype(jnp.float32), values)
        return attended.astype(jnp.bfloat16).reshape(-1, 144, chan)
    outputs = lax.map(one_row, (blocks, valid_rows))
    outputs = outputs.reshape(row_win, 2, col_win, 2, 6, 12, chan).transpose(1, 3, 0, 4, 2, 5, 6)
    return outputs.reshape(levels, rows, cols, chan)

def shifted_section(tokens, w_qkv, w_out, heads):
    lat_total = tokens.shape[1]
    normed = normalize(tokens).astype(jnp.bfloat16)
    qkv = jnp.dot(normed, w_qkv, preferred_element_type=jnp.float32).astype(jnp.bfloat16)
    qkv = jnp.roll(jnp.roll(qkv, -1, 0), -6, 2)
    qkv = jnp.pad(qkv, ((0, 0), (3, 3), (0, 0), (0, 0)))
    place = jnp.arange(lat_total + 6) - 3
    valid = (place >= 0) & (place < lat_total)
    mixed = attend_rows(qkv, valid, heads)[:, 3:lat_total + 3]
    mixed = jnp.roll(jnp.roll(mixed, 6, 2), 1, 0)
    return tokens.astype(jnp.float32) + jnp.dot(mixed, w_out, preferred_element_type=jnp.float32)

def reference(fine, fine_qkv, fine_out, fine_up, fine_down, merge_weight, coarse_qkv, coarse_out):
    hidden = shifted_section(fine, fine_qkv, fine_out, HEADS).astype(jnp.bfloat16)

    def feed(level):
        normed = normalize(level).astype(jnp.bfloat16)
        inner = jax.nn.gelu(jnp.dot(normed, fine_up, preferred_element_type=jnp.float32), approximate=False).astype(jnp.bfloat16)
        return (level.astype(jnp.float32) + jnp.dot(inner, fine_down, preferred_element_type=jnp.float32)).astype(jnp.bfloat16)
    block = lax.map(feed, hidden)
    levels, rows, cols, width = block.shape
    pairs = block.reshape(levels, rows // 2, 2, cols // 2, 2, width).transpose(0, 1, 3, 2, 4, 5)
    pairs = pairs.reshape(levels, rows // 2, cols // 2, 4 * width)
    merged = jnp.dot(normalize(pairs).astype(jnp.bfloat16), merge_weight, preferred_element_type=jnp.float32).astype(jnp.bfloat16)
    return shifted_section(merged, coarse_qkv, coarse_out, HEADS2).astype(jnp.bfloat16)
```

```python
import functools

import numpy as np
import jax
import jax.numpy as jnp
from jax import lax
from jax.experimental import pallas as pl
from jax.experimental.pallas import tpu as pltpu
from jax.sharding import PartitionSpec as P

HEADS = 16
HEADS2 = 32
ROWS = 3
COLS = 12
SEG = 2 * ROWS * COLS
LEVEL = ROWS * COLS
LANES = 128
F32 = jnp.float32
BF16 = jnp.bfloat16


def normalize(values):
    center = values - jnp.mean(values, -1, keepdims=True)
    spread = jnp.mean(center * center, -1, keepdims=True)
    return center * lax.rsqrt(spread + 1e-05)


def matmul(a, b):
    return jnp.dot(a, b, preferred_element_type=F32)


def attend(q_ref, kv_ref, out_ref, pair, lat, last, segs, heads, chan):
    size = chan // heads
    per = LANES // size
    windows = (segs + 2) // 2
    key = lax.broadcasted_iota(jnp.int32, (SEG, 2 * SEG), 1)
    query = lax.broadcasted_iota(jnp.int32, (SEG, 2 * SEG), 0)
    apart = ((key // LEVEL) % 2 != query // LEVEL) & (pair == 1)
    bias = jnp.where(apart, -1e30, 0.0)
    first = jnp.where(lat == 0, -1e30, 0.0)
    final = jnp.where(lat == last, -1e30, 0.0)
    top = jnp.minimum(bias, jnp.where(key < SEG, first, 0.0))
    bottom = jnp.minimum(bias, jnp.where(key >= SEG, final, 0.0))
    head_of = lax.broadcasted_iota(jnp.int32, (1, LANES), 1) // size
    ones = jnp.ones((2 * SEG, LANES), BF16)

    def group(g, carry):
        lane = pl.multiple_of(g * LANES, LANES)
        for w in range(windows):
            rows = pl.ds(2 * w * SEG, 2 * SEG)
            keys = kv_ref[rows, pl.ds(lane, LANES)]
            values = kv_ref[rows, pl.ds(pl.multiple_of(chan + lane, LANES), LANES)]
            values = jnp.concatenate([values, ones], 1)
            for s in (2 * w - 1, 2 * w):
                if s < 0 or s >= segs:
                    continue
                shut = top if w == 0 else bottom if w == windows - 1 else bias
                mine = pl.ds(s * SEG, SEG)
                q = q_ref[mine, pl.ds(lane, LANES)]
                total = jnp.zeros((SEG, LANES), F32)
                for h in range(per):
                    q_h = jnp.where(head_of == h, q, 0.0).astype(BF16)
                    scores = lax.dot_general(
                        q_h, keys, (((1,), (1,)), ((), ())), preferred_element_type=F32
                    ) + shut
                    expo = jnp.exp(scores - jnp.max(scores, -1, keepdims=True)).astype(BF16)
                    both = matmul(expo, values)
                    total = jnp.where(head_of == h, both[:, :LANES] / both[:, LANES:], total)
                out_ref[mine, pl.ds(lane, LANES)] = total
        return carry

    lax.fori_loop(0, chan // LANES, group, 0)


def project(x, w_ref, q_ref, kv_ref, heads, chan):
    own = q_ref.shape[0]
    normed = normalize(x)
    kv_ref[...] = matmul(normed.astype(BF16), w_ref[:, chan:]).astype(BF16)
    q_ref[...] = matmul(normed[SEG : SEG + own].astype(BF16), w_ref[:, :chan]) * (
        (chan // heads) ** -0.5
    )


def fine_kernel(col_win, x_ref, qkv_ref, out_ref, up_ref, down_ref, merge_ref, pick_ref, merged_ref,
                q_ref, kv_ref, att_ref):
    lat, last = lax.axis_index("lat"), lax.axis_size("lat") - 1
    own, chan = q_ref.shape
    x = x_ref[0].astype(F32)
    project(x, qkv_ref, q_ref, kv_ref, HEADS, chan)
    pair = pl.program_id(0) // col_win
    attend(q_ref, kv_ref, att_ref, pair, lat, last, own // SEG, HEADS, chan)
    mixed = matmul(att_ref[...].astype(BF16), out_ref[...])
    hidden = (x[SEG : SEG + own] + mixed).astype(BF16).astype(F32)
    second = normalize(hidden).astype(BF16)
    block = hidden
    width = up_ref.shape[1]
    step = 512
    for start in range(0, width, step):
        part = matmul(second, up_ref[:, start : start + step])
        inner = 0.5 * part * (1.0 + lax.erf(part * (0.5 ** 0.5)))
        block = block + matmul(inner.astype(BF16), down_ref[start : start + step, :])
    quads = matmul(pick_ref[...], block.astype(BF16))
    count = own // 4
    quads = [quads[i * count : (i + 1) * count] for i in range(4)]
    mean = sum(jnp.sum(part, -1, keepdims=True) for part in quads) / (4 * chan)
    quads = [part - mean for part in quads]
    spread = sum(jnp.sum(part * part, -1, keepdims=True) for part in quads) / (4 * chan)
    scale = lax.rsqrt(spread + 1e-05)
    merged = sum(
        matmul((part * scale).astype(BF16), merge_ref[i * chan : (i + 1) * chan, :])
        for i, part in enumerate(quads)
    )
    merged_ref[0] = merged.astype(BF16)


def coarse_kernel(x_ref, qkv_ref, out_ref, res_ref, q_ref, kv_ref, att_ref):
    lat, last = lax.axis_index("lat"), lax.axis_size("lat") - 1
    own, chan = q_ref.shape
    x = x_ref[0].astype(F32)
    project(x, qkv_ref, q_ref, kv_ref, HEADS2, chan)
    attend(q_ref, kv_ref, att_ref, pl.program_id(0), lat, last, own // SEG, HEADS2, chan)
    mixed = matmul(att_ref[...].astype(BF16), out_ref[...])
    res_ref[0] = (x[SEG : SEG + own] + mixed).astype(BF16)


def call(kernel, ext, weights, out_rows, out_width, chan, flops):
    steps, rows, width = ext.shape
    own = rows - 2 * SEG
    whole = [
        pl.BlockSpec(w.shape, lambda i: (0, 0), pipeline_mode=pl.Buffered(1)) for w in weights
    ]
    return pl.pallas_call(
        kernel,
        grid=(steps,),
        in_specs=[pl.BlockSpec((1, rows, width), lambda i: (i, 0, 0))] + whole,
        out_specs=pl.BlockSpec((1, out_rows, out_width), lambda i: (i, 0, 0)),
        out_shape=jax.ShapeDtypeStruct((steps, out_rows, out_width), BF16),
        scratch_shapes=[
            pltpu.VMEM((own, chan), F32),
            pltpu.VMEM((rows, 2 * chan), BF16),
            pltpu.VMEM((own, chan), F32),
        ],
        compiler_params=pltpu.CompilerParams(vmem_limit_bytes=48 * 2**20),
        cost_estimate=pl.CostEstimate(flops=flops, bytes_accessed=20 * 2**20, transcendentals=0),
    )(ext, *weights)


def from_next(block, axis, periodic):
    count = lax.axis_size(axis)
    pairs = [(i, i - 1) for i in range(1, count)] + ([(0, count - 1)] if periodic else [])
    return lax.ppermute(block, axis, pairs)


def from_last(block, axis, periodic):
    count = lax.axis_size(axis)
    pairs = [(i, i + 1) for i in range(count - 1)] + ([(count - 1, 0)] if periodic else [])
    return lax.ppermute(block, axis, pairs)


def widen(segments):
    low = from_last(segments[:, -1:], "lat", False)
    high = from_next(segments[:, :1], "lat", False)
    ext = jnp.concatenate([low, segments, high], 1)
    return ext.reshape(ext.shape[0], -1, ext.shape[-1])


def pick_matrix(rows):
    half = COLS // 2
    count = 2 * (rows // 2) * half
    pick = np.zeros((4 * count, 4 * count), np.float32)
    for quad in range(4):
        for r in range(count):
            level, i, j = r // (rows // 2 * half), r // half % (rows // 2), r % half
            row, col = 2 * i + quad // 2, 2 * j + quad % 2
            pick[quad * count + r, row // ROWS * SEG + level * LEVEL + row % ROWS * COLS + col] = 1
    return pick


def shards(fine, fine_qkv, fine_out, fine_up, fine_down, merge_weight, coarse_qkv, coarse_out):
    levels, rows, cols, chan = fine.shape
    col_win = cols // COLS
    shifted = jnp.concatenate([fine[:, :, 6:], from_next(fine[:, :, :6], "lon", True)], 2)
    placed = jnp.concatenate([shifted[1:], shifted[:1]], 0)
    split = placed.reshape(2, 2, rows // ROWS, ROWS, col_win, COLS, chan)
    segments = split.transpose(0, 4, 2, 1, 3, 5, 6).reshape(2 * col_win, rows // ROWS, SEG, chan)
    pick = jnp.asarray(pick_matrix(rows), BF16)
    wide = merge_weight.shape[1]
    merged = call(
        functools.partial(fine_kernel, col_win), widen(segments),
        (fine_qkv, fine_out, fine_up, fine_down, merge_weight, pick),
        rows * COLS // 2, wide, chan, 14 * 10**9,
    )
    rows2, cols2 = rows // 2, cols // 2
    merged = merged.reshape(2, col_win, 2, rows2, COLS // 2, wide).transpose(0, 2, 3, 1, 4, 5)
    merged = merged.reshape(levels, rows2, cols2, wide)
    merged = jnp.concatenate([merged[:, :, 3:], from_next(merged[:, :, :3], "lon", True)], 2)
    win2 = cols2 // COLS
    split = merged.reshape(2, 2, rows2 // ROWS, ROWS, win2, COLS, wide)
    segments = split.transpose(0, 4, 2, 1, 3, 5, 6).reshape(2 * win2, rows2 // ROWS, SEG, wide)
    coarse = call(
        coarse_kernel, widen(segments), (coarse_qkv, coarse_out),
        rows2 * 2 * COLS, wide, wide, 7 * 10**9,
    )
    coarse = coarse.reshape(2, win2, rows2 // ROWS, 2, ROWS, COLS, wide)
    coarse = coarse.transpose(0, 3, 2, 4, 1, 5, 6).reshape(levels, rows2, cols2, wide)
    coarse = jnp.concatenate([coarse[3:], coarse[:3]], 0)
    moved = from_last(coarse[:, :, cols2 - 6 :], "lon", True)
    return jnp.concatenate([moved, coarse[:, :, : cols2 - 6]], 2)


def solution(mesh):
    in_specs = (P(None, "lat", "lon", None), P(), P(), P(), P(), P(), P(), P())
    out_specs = P(None, "lat", "lon", None)
    return jax.shard_map(shards, mesh=mesh, in_specs=in_specs, out_specs=out_specs, check_vma=False)
```

```python
import functools

import numpy as np
import jax
import jax.numpy as jnp
from jax import lax
from jax.experimental import pallas as pl
from jax.experimental.pallas import tpu as pltpu
from jax.sharding import PartitionSpec as P

HEADS = 16
HEADS2 = 32
ROWS = 3
COLS = 12
SEG = 2 * ROWS * COLS
LEVEL = ROWS * COLS
LANES = 128
F32 = jnp.float32
BF16 = jnp.bfloat16


def normalize(values):
    center = values - jnp.mean(values, -1, keepdims=True)
    spread = jnp.mean(center * center, -1, keepdims=True)
    return center * lax.rsqrt(spread + 1e-05)


def matmul(a, b):
    return jnp.dot(a, b, preferred_element_type=F32)


def attend(q_ref, kv_ref, out_ref, pair, lat, last, segs, heads, chan):
    size = chan // heads
    per = LANES // size
    windows = (segs + 2) // 2
    key = lax.broadcasted_iota(jnp.int32, (SEG, 2 * SEG), 1)
    query = lax.broadcasted_iota(jnp.int32, (SEG, 2 * SEG), 0)
    apart = ((key // LEVEL) % 2 != query // LEVEL) & (pair == 1)
    bias = jnp.where(apart, -1e30, 0.0)
    first = jnp.where(lat == 0, -1e30, 0.0)
    final = jnp.where(lat == last, -1e30, 0.0)
    top = jnp.minimum(bias, jnp.where(key < SEG, first, 0.0))
    bottom = jnp.minimum(bias, jnp.where(key >= SEG, final, 0.0))
    head_of = lax.broadcasted_iota(jnp.int32, (1, LANES), 1) // size
    head_twice = lax.broadcasted_iota(jnp.int32, (1, 2 * LANES), 1) % LANES // size
    ones = jnp.ones((2 * SEG, LANES), BF16)

    def group(g, carry):
        lane = pl.multiple_of(g * LANES, LANES)
        for w in range(windows):
            rows = pl.ds(2 * w * SEG, 2 * SEG)
            keys = kv_ref[rows, pl.ds(lane, LANES)]
            values = kv_ref[rows, pl.ds(pl.multiple_of(chan + lane, LANES), LANES)]
            values = jnp.concatenate([values, ones], 1)
            segments = [s for s in (2 * w - 1, 2 * w) if 0 <= s < segs]
            shut = top if w == 0 else bottom if w == windows - 1 else bias
            count = len(segments) * SEG
            mine = pl.ds(segments[0] * SEG, count)
            q = q_ref[mine, pl.ds(lane, LANES)]
            stacked = jnp.concatenate([jnp.where(head_of == h, q, 0.0) for h in range(per)], 0)
            scores = lax.dot_general(
                stacked.astype(BF16), keys, (((1,), (1,)), ((), ())), preferred_element_type=F32
            )
            scores = scores.reshape(per * len(segments), SEG, 2 * SEG) + shut[None]
            expo = jnp.exp(scores - jnp.max(scores, -1, keepdims=True))
            both = matmul(expo.reshape(per * count, 2 * SEG).astype(BF16), values)
            total = both[:count]
            for h in range(1, per):
                part = both[h * count : (h + 1) * count]
                total = jnp.where(head_twice == h, part, total)
            out_ref[mine, pl.ds(lane, LANES)] = total[:, :LANES] / total[:, LANES:]
        return carry

    lax.fori_loop(0, chan // LANES, group, 0, unroll=2)


def project(x, w_ref, q_ref, kv_ref, heads, chan):
    own = q_ref.shape[0]
    normed = normalize(x)
    kv_ref[...] = matmul(normed.astype(BF16), w_ref[:, chan:]).astype(BF16)
    q_ref[...] = matmul(normed[SEG : SEG + own].astype(BF16), w_ref[:, :chan]) * (
        (chan // heads) ** -0.5
    )


def fine_kernel(col_win, low_ref, x_ref, high_ref, qkv_ref, out_ref, up_ref, down_ref, merge_ref, pick_ref, merged_ref,
                q_ref, kv_ref, att_ref):
    lat, last = lax.axis_index("lat"), lax.axis_size("lat") - 1
    own, chan = q_ref.shape
    x = x_ref[0].astype(F32)
    wide = [low_ref[0].astype(F32), x, high_ref[0].astype(F32)]
    project(jnp.concatenate(wide, 0), qkv_ref, q_ref, kv_ref, HEADS, chan)
    pair = pl.program_id(0) // col_win
    attend(q_ref, kv_ref, att_ref, pair, lat, last, own // SEG, HEADS, chan)
    mixed = matmul(att_ref[...].astype(BF16), out_ref[...])
    hidden = (x + mixed).astype(BF16).astype(F32)
    second = normalize(hidden).astype(BF16)
    block = hidden
    width = up_ref.shape[1]
    step = 512
    for start in range(0, width, step):
        part = matmul(second, up_ref[:, start : start + step])
        inner = 0.5 * part * (1.0 + lax.erf(part * (0.5 ** 0.5)))
        block = block + matmul(inner.astype(BF16), down_ref[start : start + step, :])
    quads = matmul(pick_ref[...], block.astype(BF16))
    count = own // 4
    quads = [quads[i * count : (i + 1) * count] for i in range(4)]
    mean = sum(jnp.sum(part, -1, keepdims=True) for part in quads) / (4 * chan)
    quads = [part - mean for part in quads]
    spread = sum(jnp.sum(part * part, -1, keepdims=True) for part in quads) / (4 * chan)
    scale = lax.rsqrt(spread + 1e-05)
    merged = sum(
        matmul((part * scale).astype(BF16), merge_ref[i * chan : (i + 1) * chan, :])
        for i, part in enumerate(quads)
    )
    merged_ref[0] = merged.astype(BF16)


def coarse_kernel(low_ref, x_ref, high_ref, qkv_ref, out_ref, res_ref, q_ref, kv_ref, att_ref):
    lat, last = lax.axis_index("lat"), lax.axis_size("lat") - 1
    own, chan = q_ref.shape
    x = x_ref[0].astype(F32)
    wide = [low_ref[0].astype(F32), x, high_ref[0].astype(F32)]
    project(jnp.concatenate(wide, 0), qkv_ref, q_ref, kv_ref, HEADS2, chan)
    attend(q_ref, kv_ref, att_ref, pl.program_id(0), lat, last, own // SEG, HEADS2, chan)
    mixed = matmul(att_ref[...].astype(BF16), out_ref[...])
    res_ref[0] = (x + mixed).astype(BF16)


def call(kernel, segments, weights, out_rows, out_width, chan, flops):
    low = from_last(segments[:, -1], "lat", False)
    high = from_next(segments[:, 0], "lat", False)
    steps, segs, _, width = segments.shape
    own = segs * SEG
    rows = own + 2 * SEG
    tokens = [low, segments.reshape(steps, own, width), high]
    pieces = [pl.BlockSpec((1,) + t.shape[1:], lambda i: (i, 0, 0)) for t in tokens]
    whole = [
        pl.BlockSpec(w.shape, lambda i: (0, 0), pipeline_mode=pl.Buffered(1)) for w in weights
    ]
    return pl.pallas_call(
        kernel,
        grid=(steps,),
        in_specs=pieces + whole,
        out_specs=pl.BlockSpec((1, out_rows, out_width), lambda i: (i, 0, 0)),
        out_shape=jax.ShapeDtypeStruct((steps, out_rows, out_width), BF16),
        scratch_shapes=[
            pltpu.VMEM((own, chan), F32),
            pltpu.VMEM((rows, 2 * chan), BF16),
            pltpu.VMEM((own, chan), F32),
        ],
        compiler_params=pltpu.CompilerParams(vmem_limit_bytes=48 * 2**20),
        cost_estimate=pl.CostEstimate(flops=flops, bytes_accessed=20 * 2**20, transcendentals=0),
    )(*tokens, *weights)


def from_next(block, axis, periodic):
    count = lax.axis_size(axis)
    pairs = [(i, i - 1) for i in range(1, count)] + ([(0, count - 1)] if periodic else [])
    return lax.ppermute(block, axis, pairs)


def from_last(block, axis, periodic):
    count = lax.axis_size(axis)
    pairs = [(i, i + 1) for i in range(count - 1)] + ([(count - 1, 0)] if periodic else [])
    return lax.ppermute(block, axis, pairs)


def pick_matrix(rows):
    half = COLS // 2
    count = 2 * (rows // 2) * half
    pick = np.zeros((4 * count, 4 * count), np.float32)
    for quad in range(4):
        for r in range(count):
            level, i, j = r // (rows // 2 * half), r // half % (rows // 2), r % half
            row, col = 2 * i + quad // 2, 2 * j + quad % 2
            pick[quad * count + r, row // ROWS * SEG + level * LEVEL + row % ROWS * COLS + col] = 1
    return pick


def shards(fine, fine_qkv, fine_out, fine_up, fine_down, merge_weight, coarse_qkv, coarse_out):
    levels, rows, cols, chan = fine.shape
    col_win = cols // COLS
    shifted = jnp.concatenate([fine[:, :, 6:], from_next(fine[:, :, :6], "lon", True)], 2)
    placed = jnp.concatenate([shifted[1:], shifted[:1]], 0)
    split = placed.reshape(2, 2, rows // ROWS, ROWS, col_win, COLS, chan)
    segments = split.transpose(0, 4, 2, 1, 3, 5, 6).reshape(2 * col_win, rows // ROWS, SEG, chan)
    pick = jnp.asarray(pick_matrix(rows), BF16)
    wide = merge_weight.shape[1]
    merged = call(
        functools.partial(fine_kernel, col_win), segments,
        (fine_qkv, fine_out, fine_up, fine_down, merge_weight, pick),
        rows * COLS // 2, wide, chan, 14 * 10**9,
    )
    rows2, cols2 = rows // 2, cols // 2
    merged = merged.reshape(2, col_win, 2, rows2, COLS // 2, wide).transpose(0, 2, 3, 1, 4, 5)
    merged = merged.reshape(levels, rows2, cols2, wide)
    merged = jnp.concatenate([merged[:, :, 3:], from_next(merged[:, :, :3], "lon", True)], 2)
    win2 = cols2 // COLS
    split = merged.reshape(2, 2, rows2 // ROWS, ROWS, win2, COLS, wide)
    segments = split.transpose(0, 4, 2, 1, 3, 5, 6).reshape(2 * win2, rows2 // ROWS, SEG, wide)
    coarse = call(
        coarse_kernel, segments, (coarse_qkv, coarse_out),
        rows2 * 2 * COLS, wide, wide, 7 * 10**9,
    )
    coarse = coarse.reshape(2, win2, rows2 // ROWS, 2, ROWS, COLS, wide)
    coarse = coarse.transpose(0, 3, 2, 4, 1, 5, 6).reshape(levels, rows2, cols2, wide)
    coarse = jnp.concatenate([coarse[3:], coarse[:3]], 0)
    moved = from_last(coarse[:, :, cols2 - 6 :], "lon", True)
    return jnp.concatenate([moved, coarse[:, :, : cols2 - 6]], 2)


def solution(mesh):
    in_specs = (P(None, "lat", "lon", None), P(), P(), P(), P(), P(), P(), P())
    out_specs = P(None, "lat", "lon", None)
    return jax.shard_map(shards, mesh=mesh, in_specs=in_specs, out_specs=out_specs, check_vma=False)
```

```python
import functools

import numpy as np
import jax
import jax.numpy as jnp
from jax import lax
from jax.experimental import pallas as pl
from jax.experimental.pallas import tpu as pltpu
from jax.sharding import PartitionSpec as P

HEADS = 16
HEADS2 = 32
ROWS = 3
COLS = 12
SEG = 2 * ROWS * COLS
LEVEL = ROWS * COLS
LANES = 128
F32 = jnp.float32
BF16 = jnp.bfloat16


def normalize(values):
    center = values - jnp.mean(values, -1, keepdims=True)
    spread = jnp.mean(center * center, -1, keepdims=True)
    return center * lax.rsqrt(spread + 1e-05)


def matmul(a, b):
    return jnp.dot(a, b, preferred_element_type=F32)


def attend(q_ref, kv_ref, out_ref, pair, lat, last, segs, heads, chan, chosen):
    size = chan // heads
    per = LANES // size
    windows = (segs + 2) // 2
    key = lax.broadcasted_iota(jnp.int32, (SEG, 2 * SEG), 1)
    query = lax.broadcasted_iota(jnp.int32, (SEG, 2 * SEG), 0)
    apart = ((key // LEVEL) % 2 != query // LEVEL) & (pair == 1)
    bias = jnp.where(apart, -1e30, 0.0)
    first = jnp.where(lat == 0, -1e30, 0.0)
    final = jnp.where(lat == last, -1e30, 0.0)
    top = jnp.minimum(bias, jnp.where(key < SEG, first, 0.0))
    bottom = jnp.minimum(bias, jnp.where(key >= SEG, final, 0.0))
    head_of = lax.broadcasted_iota(jnp.int32, (1, LANES), 1) // size
    head_twice = lax.broadcasted_iota(jnp.int32, (1, 2 * LANES), 1) % LANES // size
    ones = jnp.ones((2 * SEG, LANES), BF16)

    def group(g, carry):
        lane = pl.multiple_of(g * LANES, LANES)
        for w in chosen:
            rows = pl.ds(2 * w * SEG, 2 * SEG)
            keys = kv_ref[rows, pl.ds(lane, LANES)].astype(BF16)
            values = kv_ref[rows, pl.ds(pl.multiple_of(chan + lane, LANES), LANES)]
            values = jnp.concatenate([values.astype(BF16), ones], 1)
            segments = [s for s in (2 * w - 1, 2 * w) if 0 <= s < segs]
            shut = top if w == 0 else bottom if w == windows - 1 else bias
            count = len(segments) * SEG
            mine = pl.ds(segments[0] * SEG, count)
            q = q_ref[mine, pl.ds(lane, LANES)]
            stacked = jnp.concatenate([jnp.where(head_of == h, q, 0.0) for h in range(per)], 0)
            scores = lax.dot_general(
                stacked.astype(BF16), keys, (((1,), (1,)), ((), ())), preferred_element_type=F32
            )
            scores = scores.reshape(per * len(segments), SEG, 2 * SEG) + shut[None]
            expo = jnp.exp2(scores - jnp.max(scores, -1, keepdims=True))
            both = matmul(expo.reshape(per * count, 2 * SEG).astype(BF16), values)
            total = both[:count]
            for h in range(1, per):
                part = both[h * count : (h + 1) * count]
                total = jnp.where(head_twice == h, part, total)
            out_ref[mine, pl.ds(lane, LANES)] = total[:, :LANES] / total[:, LANES:]
        return carry

    lax.fori_loop(0, chan // LANES, group, 0, unroll=2)


def links(x_ref, halo_ref, send_sem, recv_sem, i, lat):
    segs = x_ref.shape[1]

    def copy(seg, side, device):
        return pltpu.make_async_remote_copy(
            src_ref=x_ref.at[i, seg], dst_ref=halo_ref.at[i, side],
            send_sem=send_sem.at[i, side], recv_sem=recv_sem.at[i, side],
            device_id={"lat": device}, device_id_type=pl.DeviceIdType.MESH,
        )

    return copy(segs - 1, 0, lat + 1), copy(0, 1, lat - 1)


def attention(x_ref, w_ref, q_ref, kv_ref, att_ref, halo_ref, send_sem, recv_sem, pair, heads):
    lat, last = lax.axis_index("lat"), lax.axis_size("lat") - 1
    step = pl.program_id(0)
    steps, segs, _, chan = x_ref.shape
    own = segs * SEG

    @pl.when(step == 0)
    def _():
        barrier = pltpu.get_barrier_semaphore()

        @pl.when(lat > 0)
        def _():
            pl.semaphore_signal(
                barrier, inc=1, device_id={"lat": lat - 1}, device_id_type=pl.DeviceIdType.MESH
            )

        @pl.when(lat < last)
        def _():
            pl.semaphore_signal(
                barrier, inc=1, device_id={"lat": lat + 1}, device_id_type=pl.DeviceIdType.MESH
            )

        @pl.when((lat > 0) & (lat < last))
        def _():
            pl.semaphore_wait(barrier, 2)

        @pl.when((lat == 0) | (lat == last))
        def _():
            pl.semaphore_wait(barrier, 1)

        for i in range(steps):
            down, up = links(x_ref, halo_ref, send_sem, recv_sem, i, lat)
            pl.when(lat < last)(down.start)
            pl.when(lat > 0)(up.start)

        @pl.when(lat == 0)
        def _():
            halo_ref[:, 0] = jnp.zeros((steps, SEG, chan), BF16)

        @pl.when(lat == last)
        def _():
            halo_ref[:, 1] = jnp.zeros((steps, SEG, chan), BF16)

    x = jnp.concatenate([x_ref[step, s].astype(F32) for s in range(segs)], 0)
    normed = normalize(x).astype(BF16)
    scale = (chan // heads) ** -0.5 * np.log2(np.e)
    q_ref[...] = matmul(normed, w_ref[:, :chan]) * np.float32(scale)
    kv_ref[SEG : SEG + own] = matmul(normed, w_ref[:, chan:])
    windows = (segs + 2) // 2
    inside = list(range(1, windows - 1))
    if inside:
        attend(q_ref, kv_ref, att_ref, pair, lat, last, segs, heads, chan, inside)
    down, up = links(x_ref, halo_ref, send_sem, recv_sem, step, lat)
    pl.when(lat > 0)(down.wait_recv)
    pl.when(lat < last)(up.wait_recv)
    halo = jnp.concatenate([halo_ref[step, 0].astype(F32), halo_ref[step, 1].astype(F32)], 0)
    halo = matmul(normalize(halo).astype(BF16), w_ref[:, chan:])
    kv_ref[:SEG] = halo[:SEG]
    kv_ref[SEG + own :] = halo[SEG:]
    attend(q_ref, kv_ref, att_ref, pair, lat, last, segs, heads, chan, [0, windows - 1])

    @pl.when(step == steps - 1)
    def _():
        for i in range(steps):
            down, up = links(x_ref, halo_ref, send_sem, recv_sem, i, lat)
            pl.when(lat < last)(down.wait_send)
            pl.when(lat > 0)(up.wait_send)

    return x


def fine_kernel(col_win, x_ref, qkv_ref, out_ref, up_ref, down_ref, merge_ref, pick_ref, merged_ref,
                q_ref, kv_ref, att_ref, halo_ref, send_sem, recv_sem):
    own, chan = q_ref.shape
    x = attention(x_ref, qkv_ref, q_ref, kv_ref, att_ref, halo_ref, send_sem, recv_sem,
                  pl.program_id(0) // col_win, HEADS)
    mixed = matmul(att_ref[...].astype(BF16), out_ref[...])
    hidden = (x + mixed).astype(BF16).astype(F32)
    second = normalize(hidden).astype(BF16)
    block = hidden
    width = up_ref.shape[1]
    step = 512
    for start in range(0, width, step):
        part = matmul(second, up_ref[:, start : start + step])
        inner = 0.5 * part * (1.0 + lax.erf(part * (0.5 ** 0.5)))
        block = block + matmul(inner.astype(BF16), down_ref[start : start + step, :])
    quads = matmul(pick_ref[...], block.astype(BF16))
    count = own // 4
    quads = [quads[i * count : (i + 1) * count] for i in range(4)]
    mean = sum(jnp.sum(part, -1, keepdims=True) for part in quads) / (4 * chan)
    quads = [part - mean for part in quads]
    spread = sum(jnp.sum(part * part, -1, keepdims=True) for part in quads) / (4 * chan)
    scale = lax.rsqrt(spread + 1e-05)
    merged = sum(
        matmul((part * scale).astype(BF16), merge_ref[i * chan : (i + 1) * chan, :])
        for i, part in enumerate(quads)
    )
    merged_ref[0] = merged.astype(BF16)


def coarse_kernel(win, x_ref, qkv_ref, out_ref, res_ref,
                  q_ref, kv_ref, att_ref, halo_ref, send_sem, recv_sem):
    x = attention(x_ref, qkv_ref, q_ref, kv_ref, att_ref, halo_ref, send_sem, recv_sem,
                  pl.program_id(0) // win, HEADS2)
    mixed = matmul(att_ref[...].astype(BF16), out_ref[...])
    res_ref[0] = (x + mixed).astype(BF16)


def call(kernel, segments, weights, out_rows, out_width, chan, flops, ident):
    steps, segs, _, width = segments.shape
    own = segs * SEG
    rows = own + 2 * SEG
    tokens = pl.BlockSpec(segments.shape, lambda i: (0, 0, 0, 0), pipeline_mode=pl.Buffered(1))
    whole = [
        pl.BlockSpec(w.shape, lambda i: (0, 0), pipeline_mode=pl.Buffered(1)) for w in weights
    ]
    return pl.pallas_call(
        kernel,
        grid=(steps,),
        in_specs=[tokens] + whole,
        out_specs=pl.BlockSpec((1, out_rows, out_width), lambda i: (i, 0, 0)),
        out_shape=jax.ShapeDtypeStruct((steps, out_rows, out_width), BF16),
        scratch_shapes=[
            pltpu.VMEM((own, chan), F32),
            pltpu.VMEM((rows, 2 * chan), F32),
            pltpu.VMEM((own, chan), F32),
            pltpu.VMEM((steps, 2, SEG, width), BF16),
            pltpu.SemaphoreType.DMA((steps, 2)),
            pltpu.SemaphoreType.DMA((steps, 2)),
        ],
        compiler_params=pltpu.CompilerParams(
            vmem_limit_bytes=36 * 2**20, collective_id=ident, has_side_effects=True
        ),
        cost_estimate=pl.CostEstimate(flops=flops, bytes_accessed=20 * 2**20, transcendentals=0),
    )(segments, *weights)


def from_next(block, axis, periodic):
    count = lax.axis_size(axis)
    pairs = [(i, i - 1) for i in range(1, count)] + ([(0, count - 1)] if periodic else [])
    return lax.ppermute(block, axis, pairs)


def from_last(block, axis, periodic):
    count = lax.axis_size(axis)
    pairs = [(i, i + 1) for i in range(count - 1)] + ([(count - 1, 0)] if periodic else [])
    return lax.ppermute(block, axis, pairs)


def pick_matrix(rows):
    half = COLS // 2
    count = 2 * (rows // 2) * half
    pick = np.zeros((4 * count, 4 * count), np.float32)
    for quad in range(4):
        for r in range(count):
            level, i, j = r // (rows // 2 * half), r // half % (rows // 2), r % half
            row, col = 2 * i + quad // 2, 2 * j + quad % 2
            pick[quad * count + r, row // ROWS * SEG + level * LEVEL + row % ROWS * COLS + col] = 1
    return pick


def shards(fine, fine_qkv, fine_out, fine_up, fine_down, merge_weight, coarse_qkv, coarse_out):
    levels, rows, cols, chan = fine.shape
    col_win = cols // COLS
    shifted = jnp.concatenate([fine[:, :, 6:], from_next(fine[:, :, :6], "lon", True)], 2)
    placed = jnp.concatenate([shifted[1:], shifted[:1]], 0)
    split = placed.reshape(2, 2, rows // ROWS, ROWS, col_win, COLS, chan)
    segments = split.transpose(0, 4, 2, 1, 3, 5, 6).reshape(2 * col_win, rows // ROWS, SEG, chan)
    pick = jnp.asarray(pick_matrix(rows), BF16)
    wide = merge_weight.shape[1]
    merged = call(
        functools.partial(fine_kernel, col_win), segments,
        (fine_qkv, fine_out, fine_up, fine_down, merge_weight, pick),
        rows * COLS // 2, wide, chan, 14 * 10**9, 0,
    )
    rows2, cols2 = rows // 2, cols // 2
    merged = merged.reshape(2, col_win, 2, rows2, COLS // 2, wide).transpose(0, 2, 3, 1, 4, 5)
    merged = merged.reshape(levels, rows2, cols2, wide)
    merged = jnp.concatenate([merged[:, :, 3:], from_next(merged[:, :, :3], "lon", True)], 2)
    win2 = cols2 // COLS
    split = merged.reshape(2, 2, rows2 // ROWS, ROWS, win2, COLS, wide)
    segments = split.transpose(0, 4, 2, 1, 3, 5, 6).reshape(2 * win2, rows2 // ROWS, SEG, wide)
    coarse = call(
        functools.partial(coarse_kernel, win2), segments, (coarse_qkv, coarse_out),
        rows2 * 2 * COLS, wide, wide, 7 * 10**9, 1,
    )
    coarse = coarse.reshape(2, win2, rows2 // ROWS, 2, ROWS, COLS, wide)
    coarse = coarse.transpose(0, 3, 2, 4, 1, 5, 6).reshape(levels, rows2, cols2, wide)
    coarse = jnp.concatenate([coarse[3:], coarse[:3]], 0)
    moved = from_last(coarse[:, :, cols2 - 6 :], "lon", True)
    return jnp.concatenate([moved, coarse[:, :, : cols2 - 6]], 2)


def solution(mesh):
    in_specs = (P(None, "lat", "lon", None), P(), P(), P(), P(), P(), P(), P())
    out_specs = P(None, "lat", "lon", None)
    return jax.shard_map(shards, mesh=mesh, in_specs=in_specs, out_specs=out_specs, check_vma=False)
```
